32 devices in a mesh: groups: 2 (over y), tm: 4 (over z), cols: 4 (over x, core).
Axes of the slice: x: 2, y: 2, z: 4, core: 2. Of those that a mesh axis runs over, the one named last changes fastest.
Arguments:
- latent: bfloat16 [8, 48, 128, 256], P(('groups', 'tm'), None, 'cols'), parts along dimension 0, may hold values from -6 to 6
- spatial_one: bfloat16 [3, 3, 256, 256], replicated, may hold values from -0.125 to 0.125
- bias_one: float32 [256], replicated, may hold values from -3 to 3
- spatial_two: bfloat16 [3, 3, 256, 256], replicated, may hold values from -0.125 to 0.125
- bias_two: float32 [256], replicated, may hold values from -3 to 3
- temporal_one: bfloat16 [3, 256, 256], replicated, may hold values from -0.75 to 0.75
- tbias_one: float32 [256], replicated, may hold values from -3 to 3
- temporal_two: bfloat16 [3, 256, 256], replicated, may hold values from -0.75 to 0.75
- tbias_two: float32 [256], replicated, may hold values from -3 to 3
Outputs:
- act_one: bfloat16 [8, 48, 128, 256], P(('groups', 'tm'), None, 'cols'), parts along dimension 0
- act_two: bfloat16 [8, 48, 128, 256], P(('groups', 'tm'), None, 'cols'), parts along dimension 0
- act_three: bfloat16 [8, 48, 128, 256], P(('groups', 'tm'), None, 'cols'), parts along dimension 0
- act_four: bfloat16 [8, 48, 128, 256], P(('groups', 'tm'), None, 'cols'), parts along dimension 0
The draws below stay inside these ranges and needn't reach their ends.
There are 2 independent parts, one for each index of `groups`. The reference program is written for one: setup_inputs(seed, part) draws one part's arguments, and reference() takes and returns one part's arrays. A program takes and returns all parts, laid end to end along the dimension named above; an argument that names none is the same for every part. Nothing has to cross between parts.
All inputs are finite; a program needn't handle non-finite values.
Results may differ from the reference program's by a relative error of at most 0.012.
Values may be sent and summed in bfloat16 or wider, within the bound.
A program may use at most 64 MiB of HBM per device.

```python
import math
import jax
import jax.numpy as jnp
from jax import lax

C = 256
H = 48
FRAMES = 4
W = 128


def temporal_taps(key):
    key_off, key_scale, key_sign = jax.random.split(key, 3)
    spread_off = 0.15 / math.sqrt(C)
    off_diagonal = jax.random.truncated_normal(key_off, -4.0, 4.0, (3, C, C), jnp.float32) * spread_off
    magnitude = jax.random.uniform(key_scale, (3, C), jnp.float32, 0.4, 0.6)
    sign_flip = (jax.random.randint(key_sign, (3, C), 0, 2) * 2 - 1).astype(jnp.float32)
    identity = jnp.arange(C)[:, None] == jnp.arange(C)[None, :]
    diagonal = (sign_flip * magnitude)[:, :, None]
    return jnp.where(identity[None, :, :], diagonal, off_diagonal).astype(jnp.bfloat16)


def draw_temporal_one(key, part):
    return temporal_taps(jax.random.fold_in(key, 11))


def draw_temporal_two(key, part):
    return temporal_taps(jax.random.fold_in(key, 23))


def block_levels(rng, shape, shards, smallest, high):
    def one(axis_at, parts):
        heights = jax.random.uniform(jax.random.fold_in(jax.random.fold_in(rng, 6), axis_at), (parts,), jnp.float32, smallest / len(shards), high / len(shards))
        return jnp.repeat(jnp.exp(heights), shape[axis_at] // parts).reshape((-1,) + (1,) * (len(shape) - axis_at - 1))

    loudness = one(*shards[0])
    for cut in shards[1:]:
        loudness = loudness * one(*cut)
    return loudness


def bell_draw(key, dims, spread, most, cuts=(), kind=jnp.bfloat16):
    factor_of = block_levels(key, dims, cuts, -0.22, 0.18) if cuts else 1.0
    result = jax.random.normal(key, dims, jnp.float32) * spread * factor_of
    return jnp.minimum(jnp.maximum(result, -most), most).astype(kind)


def setup_inputs(seed: int = 0, part: int = 0) -> dict:
    key_of = jax.random.split(jax.random.key(seed), 10)
    part_keys = jax.random.split(jax.random.fold_in(key_of[9], part), 10)
    latent = bell_draw(part_keys[0], (FRAMES, H, W, C), 1.0, 6.0, ((0, 4), (2, 4)))
    spatial_one = bell_draw(key_of[1], (3, 3, C, C), (9 * C) ** -0.5, 0.125)
    bias_one = bell_draw(key_of[2], (C,), 0.5, 3.0, (), jnp.float32)
    spatial_two = bell_draw(key_of[3], (3, 3, C, C), (9 * C) ** -0.5, 0.125)
    bias_two = bell_draw(key_of[4], (C,), 0.5, 3.0, (), jnp.float32)
    temporal_one = draw_temporal_one(jax.random.fold_in(key_of[9], 71), part)
    tbias_one = bell_draw(key_of[6], (C,), 0.5, 3.0, (), jnp.float32)
    temporal_two = draw_temporal_two(jax.random.fold_in(key_of[9], 71), part)
    tbias_two = bell_draw(key_of[8], (C,), 0.5, 3.0, (), jnp.float32)
    return dict(latent=latent, spatial_one=spatial_one, bias_one=bias_one, spatial_two=spatial_two, bias_two=bias_two, temporal_one=temporal_one, tbias_one=tbias_one, temporal_two=temporal_two, tbias_two=tbias_two)


def silu_round(values):
    return jax.nn.silu(values.astype(jnp.float32)).astype(jnp.bfloat16)


def spatial_layer(inputs, kernel, bias):
    rows, width, chans = inputs.shape[1], inputs.shape[2], inputs.shape[3]
    flat_kernel = kernel.reshape(9 * chans, chans)

    def one_frame(frame):
        activated = silu_round(frame)
        padded = jnp.pad(activated, ((1, 1), (1, 1), (0, 0)))
        taps = [padded[dr:dr + rows, dc:dc + width, :] for dr in range(3) for dc in range(3)]
        stacked = jnp.concatenate(taps, axis=-1).reshape(rows * width, 9 * chans)
        conv = jnp.dot(stacked, flat_kernel, preferred_element_type=jnp.float32).reshape(rows, width, chans)
        return (frame.astype(jnp.float32) + conv + bias.astype(jnp.float32)).astype(jnp.bfloat16)

    return lax.map(one_frame, inputs)


def causal_layer(inputs, kernel, bias):
    frames, chans = inputs.shape[0], inputs.shape[3]
    activated = silu_round(inputs)
    padded = jnp.pad(activated, ((2, 0), (0, 0), (0, 0), (0, 0)))
    stacked = jnp.concatenate([padded[0:frames], padded[1:frames + 1], padded[2:frames + 2]], axis=-1)
    conv = jnp.dot(stacked.reshape(-1, 3 * chans), kernel.reshape(3 * chans, chans), preferred_element_type=jnp.float32)
    conv = conv.reshape(inputs.shape)
    return (inputs.astype(jnp.float32) + conv + bias.astype(jnp.float32)).astype(jnp.bfloat16)


def reference(latent, spatial_one, bias_one, spatial_two, bias_two, temporal_one, tbias_one, temporal_two, tbias_two):
    act_one = spatial_layer(latent, spatial_one, bias_one)
    act_two = spatial_layer(act_one, spatial_two, bias_two)
    act_three = causal_layer(act_two, temporal_one, tbias_one)
    act_four = causal_layer(act_three, temporal_two, tbias_two)
    return (act_one, act_two, act_three, act_four)
```

```python
import functools

import jax
import jax.numpy as jnp
from jax import lax
from jax.experimental import pallas as pl
from jax.experimental.pallas import tpu as pltpu
from jax.sharding import PartitionSpec as P

MESH = pl.DeviceIdType.MESH
TILE = 16
LAG = 2


def silu(values):
    half = 0.5 * values.astype(jnp.float32)
    return half + half * jnp.tanh(half)


def mm(a, b):
    return jnp.dot(a, b, preferred_element_type=jnp.float32)


def kernel(
    n, n_cols, R, hops,
    x_ref, k1, b1, k2, b2, u, tb1, v, tb2,
    o1, o2, o3, o4,
    hal1, hal2, s1, s2, a1, a2, a3, a4, x2in, qs, ps, qr, pr,
    h_send, h_recv, z_send, z_recv, q_send, q_recv, o_sem,
):
    k = lax.axis_index("tm")
    c = lax.axis_index("cols")
    rows, W, C = a1.shape
    chunks = rows // R
    M = R * W
    last = n - 1
    x = x_ref.at[0]

    def cut(j):
        return pl.ds(j * R, R)

    partners = [(c > 0, {"cols": c - 1}), (c < n_cols - 1, {"cols": c + 1})]
    for h in range(1, hops + 1):
        partners.append((k + h < last, {"tm": k + h}))
        partners.append(((k - h >= 0) & (k < last), {"tm": k - h}))
    if n > 1:
        partners.append((k == last - 1, {"tm": k + 1}))
        partners.append((k == last, {"tm": k - 1}))
    barrier = pltpu.get_barrier_semaphore()
    count = jnp.int32(0)
    for there, device in partners:
        count = count + there.astype(jnp.int32)

        @pl.when(there)
        def _():
            pl.semaphore_signal(barrier, inc=1, device_id=device, device_id_type=MESH)

    edge = jnp.zeros((rows, TILE, C), jnp.bfloat16)

    @pl.when(c == 0)
    def _():
        hal1[0] = edge
        hal2[0] = edge

    @pl.when(c == n_cols - 1)
    def _():
        hal1[1] = edge
        hal2[1] = edge

    for s in (s1, s2):
        s[0] = jnp.zeros(s.shape[1:], s.dtype)
        s[rows + 1] = jnp.zeros(s.shape[1:], s.dtype)
    for h in range(1, hops + 1):

        @pl.when((k < h) & (k < last))
        def _():
            x2in[h - 1] = jnp.zeros(x2in.shape[1:], x2in.dtype)

    pl.semaphore_wait(barrier, count)

    def halo(layer, side, j):
        src = a1 if layer else x
        dst = hal2 if layer else hal1
        tile = pl.ds(W - TILE, TILE) if side == 0 else pl.ds(0, TILE)
        return pltpu.make_async_remote_copy(
            src_ref=src.at[cut(j), tile, :],
            dst_ref=dst.at[side, cut(j)],
            send_sem=h_send.at[layer, side, j],
            recv_sem=h_recv.at[layer, side, j],
            device_id={"cols": c + 1 if side == 0 else c - 1},
            device_id_type=MESH,
        )

    def halo_sends(layer, j, act):
        @pl.when(c < n_cols - 1)
        def _():
            act(halo(layer, 0, j))

        @pl.when(c > 0)
        def _():
            act(halo(layer, 1, j))

    def halo_waits(layer, j):
        @pl.when(c > 0)
        def _():
            halo(layer, 0, j).wait_recv()

        @pl.when(c < n_cols - 1)
        def _():
            halo(layer, 1, j).wait_recv()

    def frame_copy(h, j):
        return pltpu.make_async_remote_copy(
            src_ref=a2.at[cut(j)],
            dst_ref=x2in.at[h - 1, cut(j)],
            send_sem=z_send.at[h - 1, j],
            recv_sem=z_recv.at[h - 1, j],
            device_id={"tm": k + h},
            device_id_type=MESH,
        )

    def frame_sends(j, act):
        for h in range(1, hops + 1):

            @pl.when(k + h < last)
            def _():
                act(frame_copy(h, j))

    def part_copy(which, j):
        return pltpu.make_async_remote_copy(
            src_ref=(ps if which else qs).at[cut(j)],
            dst_ref=(pr if which else qr).at[cut(j)],
            send_sem=q_send.at[which, j],
            recv_sem=q_recv.at[which, j],
            device_id={"tm": k + 1},
            device_id_type=MESH,
        )

    def out_copy(which, j):
        src, dst = ((a1, o1), (a2, o2), (a3, o3), (a4, o4))[which]
        return pltpu.make_async_copy(src.at[cut(j)], dst.at[0, cut(j)], o_sem.at[which, j])

    def build(layer, j):
        src, hal, dst = (a1, hal2, s2) if layer else (x, hal1, s1)
        mid = silu(src[cut(j)])
        left = silu(hal[0, cut(j)][:, TILE - 1 :, :])
        right = silu(hal[1, cut(j)][:, :1, :])
        here = pl.ds(j * R + 1, R)
        dst[here, :, 0:C] = jnp.concatenate([left, mid[:, : W - 1]], axis=1).astype(jnp.bfloat16)
        dst[here, :, C : 2 * C] = mid.astype(jnp.bfloat16)
        dst[here, :, 2 * C : 3 * C] = jnp.concatenate([mid[:, 1:], right], axis=1).astype(jnp.bfloat16)

    def conv(layer, j):
        src, s, kern, bias, dst = (a1, s2, k2, b2, a2) if layer else (x, s1, k1, b1, a1)
        acc = src[cut(j)].reshape(M, C).astype(jnp.float32) + bias[...][None, :]
        for dr in range(3):
            acc = acc + mm(s[pl.ds(j * R + dr, R)].reshape(M, 3 * C), kern[dr])
        dst[cut(j)] = acc.astype(jnp.bfloat16).reshape(R, W, C)

    def load(ref):
        return ref.reshape(M, C)

    def act(values):
        return silu(values).astype(jnp.bfloat16)

    def temporal_own(j):
        for h in range(1, hops + 1):

            @pl.when(k >= h)
            def _():
                frame_copy(h, j).wait_recv()

        x2 = [load(a2[cut(j)])] + [load(x2in[h - 1, cut(j)]) for h in range(1, hops + 1)]
        t2 = [act(values) for values in x2]
        if n > 2:
            first = mm(t2[0], u[1]) + mm(t2[1], u[0])
        else:
            first = mm(t2[0], u[1])

        @pl.when(k == last - 1)
        def _():
            qs[cut(j)] = first.astype(jnp.bfloat16).reshape(R, W, C)
            part_copy(0, j).start()

        x3 = []
        for i in range(min(3, hops + 1)):
            total = x2[i].astype(jnp.float32) + tb1[...][None, :]
            for tap in range(3):
                if i + tap <= hops:
                    total = total + mm(t2[i + tap], u[2 - tap])
            if i > 0:
                total = jnp.where(k >= i, total, 0.0)
            x3.append(total.astype(jnp.bfloat16))
        a3[cut(j)] = x3[0].reshape(R, W, C)
        out_copy(2, j).start()
        t3 = [act(values) for values in x3]

        @pl.when(k == last - 1)
        def _():
            second = mm(t3[0], v[1])
            if len(t3) > 1:
                second = second + mm(t3[1], v[0])
            ps[cut(j)] = second.astype(jnp.bfloat16).reshape(R, W, C)
            part_copy(1, j).start()

        total = x3[0].astype(jnp.float32) + tb2[...][None, :]
        for tap in range(len(t3)):
            total = total + mm(t3[tap], v[2 - tap])
        a4[cut(j)] = total.astype(jnp.bfloat16).reshape(R, W, C)
        out_copy(3, j).start()

    def temporal_last(j):
        x2 = load(a2[cut(j)])
        total = x2.astype(jnp.float32) + mm(act(x2), u[2]) + tb1[...][None, :]
        if n > 1:
            part_copy(0, j).wait_recv()
            total = total + load(qr[cut(j)]).astype(jnp.float32)
        x3 = total.astype(jnp.bfloat16)
        a3[cut(j)] = x3.reshape(R, W, C)
        out_copy(2, j).start()
        total = x3.astype(jnp.float32) + mm(act(x3), v[2]) + tb2[...][None, :]
        if n > 1:
            part_copy(1, j).wait_recv()
            total = total + load(pr[cut(j)]).astype(jnp.float32)
        a4[cut(j)] = total.astype(jnp.bfloat16).reshape(R, W, C)
        out_copy(3, j).start()

    def start(copy):
        copy.start()

    @pl.loop(0, chunks)
    def _(j):
        halo_sends(0, j, start)

    def during(j, body):
        @pl.when((j >= 0) & (j < chunks))
        def _():
            body(j)

    def step_build1(j):
        halo_waits(0, j)
        build(0, j)

    def step_conv1(j):
        conv(0, j)
        halo_sends(1, j, start)
        out_copy(0, j).start()

    def step_build2(j):
        halo_waits(1, j)
        build(1, j)

    def step_conv2(j):
        conv(1, j)
        frame_sends(j, start)
        out_copy(1, j).start()

    def step_temporal(j):
        @pl.when(k < last)
        def _():
            temporal_own(j)

        @pl.when(k == last)
        def _():
            temporal_last(j)

    @pl.loop(0, chunks + 3 + LAG)
    def _(t):
        during(t, step_build1)
        during(t - 1, step_conv1)
        during(t - 2, step_build2)
        during(t - 3, step_conv2)
        during(t - 3 - LAG, step_temporal)

    @pl.loop(0, chunks)
    def _(j):
        for layer in range(2):
            halo_sends(layer, j, lambda copy: copy.wait_send())
        frame_sends(j, lambda copy: copy.wait_send())
        for which in range(4):
            out_copy(which, j).wait()
        if n > 1:

            @pl.when(k == last - 1)
            def _():
                part_copy(0, j).wait_send()
                part_copy(1, j).wait_send()


def rows_per_chunk(rows):
    return max(r for r in range(1, 9) if rows % r == 0)


def on_device(n, n_cols, latent, spatial_one, bias_one, spatial_two, bias_two, temporal_one, tbias_one, temporal_two, tbias_two):
    _, rows, W, C = latent.shape
    R = rows_per_chunk(rows)
    chunks = rows // R
    hops = max(0, min(4, n - 2))
    slots = max(1, hops)
    bf = jnp.bfloat16
    block = pltpu.VMEM((rows, W, C), bf)
    dma = pltpu.SemaphoreType.DMA
    whole = pl.BlockSpec(memory_space=pltpu.VMEM)
    out = jax.ShapeDtypeStruct(latent.shape, bf)
    return pl.pallas_call(
        functools.partial(kernel, n, n_cols, R, hops),
        out_shape=(out,) * 4,
        in_specs=[whole] * 9,
        out_specs=(pl.BlockSpec(memory_space=pl.ANY),) * 4,
        scratch_shapes=[
            pltpu.VMEM((2, rows, TILE, C), bf),
            pltpu.VMEM((2, rows, TILE, C), bf),
            pltpu.VMEM((rows + 2, W, 3 * C), bf),
            pltpu.VMEM((rows + 2, W, 3 * C), bf),
            block, block, block, block,
            pltpu.VMEM((slots, rows, W, C), bf),
            block, block, block, block,
            dma((2, 2, chunks)), dma((2, 2, chunks)),
            dma((slots, chunks)), dma((slots, chunks)),
            dma((2, chunks)), dma((2, chunks)),
            dma((4, chunks)),
        ],
        compiler_params=pltpu.CompilerParams(
            collective_id=0, has_side_effects=True, vmem_limit_bytes=48 * 1024 * 1024
        ),
    )(
        latent,
        spatial_one.reshape(3, 3 * C, C), bias_one,
        spatial_two.reshape(3, 3 * C, C), bias_two,
        temporal_one, tbias_one, temporal_two, tbias_two,
    )


def solution(mesh):
    spec = P(("groups", "tm"), None, "cols", None)
    return jax.shard_map(
        functools.partial(on_device, mesh.shape["tm"], mesh.shape["cols"]),
        mesh=mesh,
        in_specs=(spec, P(), P(), P(), P(), P(), P(), P(), P()),
        out_specs=(spec,) * 4,
        check_vma=False,
    )
```

```python
import functools

import jax
import jax.numpy as jnp
from jax import lax
from jax.experimental import pallas as pl
from jax.experimental.pallas import tpu as pltpu
from jax.sharding import PartitionSpec as P

MESH = pl.DeviceIdType.MESH
TILE = 16
LAG = 3
EARLY = 0
HALO_LAG = 2
ROWS = 4
PIECES = 2
VMEM_BYTES = 58 * 1024 * 1024


def silu(values):
    half = 0.5 * values.astype(jnp.float32)
    return half + half * jnp.tanh(half)


def mm(a, b):
    return jnp.dot(a, b, preferred_element_type=jnp.float32)


def kernel(
    n, n_cols, R, hops,
    *refs,
):
    given, outs, held = refs[:9], refs[9:13], refs[13:22]
    hal1, hal2, s1, s2, x2in, qs, ps, qr, pr, a1, a2, a3, a4 = refs[22:35]
    h_send, h_recv, z_send, z_recv, q_send, q_recv, i_sem, o_sem = refs[35:]
    x_held, k1, b1, k2, b2, u, tb1, v, tb2 = held

    k = lax.axis_index("tm")
    c = lax.axis_index("cols")
    rows, W, C = a1.shape
    loads = [pltpu.make_async_copy(given[i], held[i], i_sem.at[i]) for i in range(9)]
    for load_in in loads:
        load_in.start()
    chunks = rows // R
    M = R * W
    last = n - 1
    x = x_held.at[0]
    x_hbm = given[0].at[0]

    def cut(j):
        return pl.ds(j * R, R)

    partners = [(c > 0, {"cols": c - 1}), (c < n_cols - 1, {"cols": c + 1})]
    for h in range(1, hops + 1):
        partners.append((k + h < last, {"tm": k + h}))
        partners.append(((k - h >= 0) & (k < last), {"tm": k - h}))
    if n > 1:
        partners.append((k == last - 1, {"tm": k + 1}))
        partners.append((k == last, {"tm": k - 1}))
    barrier = pltpu.get_barrier_semaphore()
    count = jnp.int32(0)
    for there, device in partners:
        count = count + there.astype(jnp.int32)

        @pl.when(there)
        def _():
            pl.semaphore_signal(barrier, inc=1, device_id=device, device_id_type=MESH)

    edge = jnp.zeros((rows, TILE, C), jnp.bfloat16)

    @pl.when(c == 0)
    def _():
        hal1[0] = edge
        hal2[0] = edge

    @pl.when(c == n_cols - 1)
    def _():
        hal1[1] = edge
        hal2[1] = edge

    for s in (s1, s2):
        s[0] = jnp.zeros(s.shape[1:], s.dtype)
        s[rows + 1] = jnp.zeros(s.shape[1:], s.dtype)
    for h in range(1, hops + 1):

        @pl.when((k < h) & (k < last))
        def _():
            x2in[h - 1] = jnp.zeros(x2in.shape[1:], x2in.dtype)

    pl.semaphore_wait(barrier, count)

    def halo(layer, side, j):
        src = a1 if layer else x_hbm
        dst = hal2 if layer else hal1
        tile = pl.ds(W - TILE, TILE) if side == 0 else pl.ds(0, TILE)
        return pltpu.make_async_remote_copy(
            src_ref=src.at[cut(j), tile, :],
            dst_ref=dst.at[side, cut(j)],
            send_sem=h_send.at[layer, side, j],
            recv_sem=h_recv.at[layer, side, j],
            device_id={"cols": c + 1 if side == 0 else c - 1},
            device_id_type=MESH,
        )

    def halo_sends(layer, j, act):
        @pl.when(c < n_cols - 1)
        def _():
            act(halo(layer, 0, j))

        @pl.when(c > 0)
        def _():
            act(halo(layer, 1, j))

    def halo_waits(layer, j):
        @pl.when(c > 0)
        def _():
            halo(layer, 0, j).wait_recv()

        @pl.when(c < n_cols - 1)
        def _():
            halo(layer, 1, j).wait_recv()

    def frame_copy(h, j):
        return pltpu.make_async_remote_copy(
            src_ref=a2.at[cut(j)],
            dst_ref=x2in.at[h - 1, cut(j)],
            send_sem=z_send.at[h - 1, j],
            recv_sem=z_recv.at[h - 1, j],
            device_id={"tm": k + h},
            device_id_type=MESH,
        )

    def frame_sends(j, act):
        for h in range(1, hops + 1):

            @pl.when(k + h < last)
            def _():
                act(frame_copy(h, j))

    def part_copy(which, j):
        return pltpu.make_async_remote_copy(
            src_ref=(ps if which else qs).at[cut(j)],
            dst_ref=(pr if which else qr).at[cut(j)],
            send_sem=q_send.at[which, j],
            recv_sem=q_recv.at[which, j],
            device_id={"tm": k + 1},
            device_id_type=MESH,
        )

    def out_copy(which, j):
        src = (a1, a2, a3, a4)[which]
        return pltpu.make_async_copy(src.at[cut(j)], outs[which].at[0, cut(j)], o_sem.at[which, j])

    def build(layer, j):
        src, hal, dst = (a1, hal2, s2) if layer else (x, hal1, s1)
        mid = silu(src[cut(j)])
        left = silu(hal[0, cut(j)][:, TILE - 1 :, :])
        right = silu(hal[1, cut(j)][:, :1, :])
        here = pl.ds(j * R + 1, R)
        dst[here, :, 0:C] = jnp.concatenate([left, mid[:, : W - 1]], axis=1).astype(jnp.bfloat16)
        dst[here, :, C : 2 * C] = mid.astype(jnp.bfloat16)
        dst[here, :, 2 * C : 3 * C] = jnp.concatenate([mid[:, 1:], right], axis=1).astype(jnp.bfloat16)

    def conv(layer, j):
        src, s, kern, bias, dst = (a1, s2, k2, b2, a2) if layer else (x, s1, k1, b1, a1)
        acc = src[cut(j)].reshape(M, C).astype(jnp.float32) + bias[...][None, :]
        for dr in range(3):
            acc = acc + mm(s[pl.ds(j * R + dr, R)].reshape(M, 3 * C), kern[dr])
        dst[cut(j)] = acc.astype(jnp.bfloat16).reshape(R, W, C)

    def load(ref):
        return ref.reshape(M, C)

    def act(values):
        return silu(values).astype(jnp.bfloat16)

    def temporal_own(j):
        def arrive(h):
            @pl.when(k >= h)
            def _():
                frame_copy(h, j).wait_recv()

        x2 = [load(a2[cut(j)])]
        if hops > 0:
            arrive(1)
            x2.append(load(x2in[0, cut(j)]))
        t2 = [act(values) for values in x2]

        @pl.when(k == last - 1)
        def _():
            part = mm(t2[0], u[1])
            if hops > 0:
                part = part + mm(t2[1], u[0])
            qs[cut(j)] = part.astype(jnp.bfloat16).reshape(R, W, C)
            part_copy(0, j).start()

        for h in range(2, hops + 1):
            arrive(h)
            x2.append(load(x2in[h - 1, cut(j)]))
            t2.append(act(x2[h]))
        x3 = []
        for i in range(min(3, hops + 1)):
            total = x2[i].astype(jnp.float32) + tb1[...][None, :]
            for tap in range(3):
                if i + tap <= hops:
                    total = total + mm(t2[i + tap], u[2 - tap])
            if i > 0:
                total = jnp.where(k >= i, total, 0.0)
            x3.append(total.astype(jnp.bfloat16))
        t3 = [act(values) for values in x3]

        @pl.when(k == last - 1)
        def _():
            part = mm(t3[0], v[1])
            if len(t3) > 1:
                part = part + mm(t3[1], v[0])
            ps[cut(j)] = part.astype(jnp.bfloat16).reshape(R, W, C)
            part_copy(1, j).start()

        a3[cut(j)] = x3[0].reshape(R, W, C)
        out_copy(2, j).start()
        total = x3[0].astype(jnp.float32) + tb2[...][None, :]
        for tap in range(len(t3)):
            total = total + mm(t3[tap], v[2 - tap])
        a4[cut(j)] = total.astype(jnp.bfloat16).reshape(R, W, C)
        out_copy(3, j).start()

    def temporal_last(j):
        x2 = load(a2[cut(j)])
        total = x2.astype(jnp.float32) + mm(act(x2), u[2]) + tb1[...][None, :]
        if n > 1:
            part_copy(0, j).wait_recv()
            total = total + load(qr[cut(j)]).astype(jnp.float32)
        x3 = total.astype(jnp.bfloat16)
        a3[cut(j)] = x3.reshape(R, W, C)
        out_copy(2, j).start()
        total = x3.astype(jnp.float32) + mm(act(x3), v[2]) + tb2[...][None, :]
        if n > 1:
            part_copy(1, j).wait_recv()
            total = total + load(pr[cut(j)]).astype(jnp.float32)
        a4[cut(j)] = total.astype(jnp.bfloat16).reshape(R, W, C)
        out_copy(3, j).start()

    def start(copy):
        copy.start()

    @pl.loop(0, chunks)
    def _(j):
        halo_sends(0, j, start)

    def during(j, body):
        @pl.when((j >= 0) & (j < chunks))
        def _():
            body(j)

    def step_build1(j):
        halo_waits(0, j)
        build(0, j)

    def step_conv1(j):
        conv(0, j)
        halo_sends(1, j, start)
        out_copy(0, j).start()

    def step_build2(j):
        halo_waits(1, j)
        build(1, j)

    def step_conv2(j):
        conv(1, j)
        frame_sends(j, start)
        out_copy(1, j).start()

    def step_temporal(j):
        @pl.when(k < last)
        def _():
            temporal_own(j)

        @pl.when(k == last)
        def _():
            temporal_last(j)

    for load_in in loads:
        load_in.wait()
    lag = jnp.where(k == last - 1, EARLY, LAG)

    @pl.loop(0, chunks + 2 + HALO_LAG + LAG)
    def _(t):
        during(t, step_build1)
        during(t - 1, step_conv1)
        during(t - 1 - HALO_LAG, step_build2)
        during(t - 2 - HALO_LAG, step_conv2)
        during(t - 2 - HALO_LAG - lag, step_temporal)

    @pl.loop(0, chunks)
    def _(j):
        for layer in range(2):
            halo_sends(layer, j, lambda copy: copy.wait_send())
        frame_sends(j, lambda copy: copy.wait_send())
        for which in range(4):
            out_copy(which, j).wait()
        if n > 1:

            @pl.when(k == last - 1)
            def _():
                part_copy(0, j).wait_send()
                part_copy(1, j).wait_send()


def rows_per_chunk(rows):
    return max(r for r in range(1, ROWS + 1) if rows % r == 0)


def on_device(n, n_cols, latent, spatial_one, bias_one, spatial_two, bias_two, temporal_one, tbias_one, temporal_two, tbias_two):
    _, rows, W, C = latent.shape
    R = rows_per_chunk(rows)
    chunks = rows // R
    hops = max(0, min(4, n - 2))
    slots = max(1, hops)
    bf = jnp.bfloat16
    block = pltpu.VMEM((rows, W, C), bf)
    dma = pltpu.SemaphoreType.DMA
    anywhere = pl.BlockSpec(memory_space=pl.ANY)
    out = jax.ShapeDtypeStruct(latent.shape, bf)
    args = (
        latent,
        spatial_one.reshape(3, 3 * C, C), bias_one,
        spatial_two.reshape(3, 3 * C, C), bias_two,
        temporal_one, tbias_one, temporal_two, tbias_two,
    )
    results = pl.pallas_call(
        functools.partial(kernel, n, n_cols, R, hops),
        out_shape=(out,) * 4,
        in_specs=[anywhere] * 9,
        out_specs=(anywhere,) * 4,
        scratch_shapes=[
            *(pltpu.VMEM(arg.shape, arg.dtype) for arg in args),
            pltpu.VMEM((2, rows, TILE, C), bf),
            pltpu.VMEM((2, rows, TILE, C), bf),
            pltpu.VMEM((rows + 2, W, 3 * C), bf),
            pltpu.VMEM((rows + 2, W, 3 * C), bf),
            pltpu.VMEM((slots, rows, W, C), bf),
            block, block, block, block,
            block, block, block, block,
            dma((2, 2, chunks)), dma((2, 2, chunks)),
            dma((slots, chunks)), dma((slots, chunks)),
            dma((2, chunks)), dma((2, chunks)),
            dma((9,)), dma((4, chunks)),
        ],
        compiler_params=pltpu.CompilerParams(
            collective_id=0, has_side_effects=True, vmem_limit_bytes=VMEM_BYTES
        ),
    )(*args)
    return pl.pallas_call(
        write_out,
        out_shape=(out,) * 4,
        in_specs=[anywhere] * 4,
        out_specs=(anywhere,) * 4,
        scratch_shapes=[
            *(pltpu.VMEM(latent.shape, bf) for _ in range(4)),
            dma((4, PIECES)), dma((4, PIECES)),
        ],
        compiler_params=pltpu.CompilerParams(vmem_limit_bytes=VMEM_BYTES),
    )(*results)


def write_out(*refs):
    given, outs, held, i_sem, o_sem = refs[:4], refs[4:8], refs[8:12], refs[12], refs[13]
    rows = given[0].shape[1]
    ins, back = [], []
    for p in range(PIECES):
        part = pl.ds(rows * p // PIECES, rows * (p + 1) // PIECES - rows * p // PIECES)
        for i in range(4):
            ins.append(pltpu.make_async_copy(given[i].at[:, part], held[i].at[:, part], i_sem.at[i, p]))
            back.append(pltpu.make_async_copy(held[i].at[:, part], outs[i].at[:, part], o_sem.at[i, p]))
    for copy in ins:
        copy.start()
    for copy, after in zip(ins, back):
        copy.wait()
        after.start()
    for copy in back:
        copy.wait()


def solution(mesh):
    spec = P(("groups", "tm"), None, "cols", None)
    return jax.shard_map(
        functools.partial(on_device, mesh.shape["tm"], mesh.shape["cols"]),
        mesh=mesh,
        in_specs=(spec, P(), P(), P(), P(), P(), P(), P(), P()),
        out_specs=(spec,) * 4,
        check_vma=False,
    )
```

```python
import functools

import jax
import jax.numpy as jnp
from jax import lax
from jax.experimental import pallas as pl
from jax.experimental.pallas import tpu as pltpu
from jax.sharding import PartitionSpec as P

MESH = pl.DeviceIdType.MESH
TILE = 16
LAG = 3
EARLY = 0
HALO_LAG = 2
ROWS = 4
PIECES = 2
VMEM_BYTES = 58 * 1024 * 1024


def silu(values):
    half = 0.5 * values.astype(jnp.float32)
    return half + half * jnp.tanh(half)


def mm(a, b):
    return jnp.dot(a, b, preferred_element_type=jnp.float32)


def kernel(
    n, n_cols, R, hops,
    *refs,
):
    given, outs, held = refs[:9], refs[9:13], refs[13:22]
    hal1, hal2, s1, s2, x2in, qs, ps, qr, pr, a1, a2, a3, a4 = refs[22:35]
    h_send, h_recv, z_send, z_recv, q_send, q_recv, i_sem, o_sem = refs[35:]
    x_held, k1, b1, k2, b2, u, tb1, v, tb2 = held

    k = lax.axis_index("tm")
    c = lax.axis_index("cols")
    rows, W, C = a1.shape
    loads = [pltpu.make_async_copy(given[i], held[i], i_sem.at[i]) for i in range(9)]
    for load_in in loads:
        load_in.start()
    chunks = rows // R
    M = R * W
    last = n - 1
    x = x_held.at[0]
    x_hbm = given[0].at[0]

    def cut(j):
        return pl.ds(j * R, R)

    partners = [(c > 0, {"cols": c - 1}), (c < n_cols - 1, {"cols": c + 1})]
    for h in range(1, hops + 1):
        partners.append((k + h < last, {"tm": k + h}))
        partners.append(((k - h >= 0) & (k < last), {"tm": k - h}))
    if n > 1:
        partners.append((k == last - 1, {"tm": k + 1}))
        partners.append((k == last, {"tm": k - 1}))
    barrier = pltpu.get_barrier_semaphore()
    count = jnp.int32(0)
    for there, device in partners:
        count = count + there.astype(jnp.int32)

        @pl.when(there)
        def _():
            pl.semaphore_signal(barrier, inc=1, device_id=device, device_id_type=MESH)

    edge = jnp.zeros((rows, TILE, C), jnp.bfloat16)

    @pl.when(c == 0)
    def _():
        hal1[0] = edge
        hal2[0] = edge

    @pl.when(c == n_cols - 1)
    def _():
        hal1[1] = edge
        hal2[1] = edge

    for s in (s1, s2):
        s[0] = jnp.zeros(s.shape[1:], s.dtype)
        s[rows + 1] = jnp.zeros(s.shape[1:], s.dtype)
    for h in range(1, hops + 1):

        @pl.when((k < h) & (k < last))
        def _():
            x2in[h - 1] = jnp.zeros(x2in.shape[1:], x2in.dtype)

    pl.semaphore_wait(barrier, count)

    def halo(layer, side, j):
        src = a1 if layer else x_hbm
        dst = hal2 if layer else hal1
        tile = pl.ds(W - TILE, TILE) if side == 0 else pl.ds(0, TILE)
        return pltpu.make_async_remote_copy(
            src_ref=src.at[cut(j), tile, :],
            dst_ref=dst.at[side, cut(j)],
            send_sem=h_send.at[layer, side, j],
            recv_sem=h_recv.at[layer, side, j],
            device_id={"cols": c + 1 if side == 0 else c - 1},
            device_id_type=MESH,
        )

    def halo_sends(layer, j, act):
        @pl.when(c < n_cols - 1)
        def _():
            act(halo(layer, 0, j))

        @pl.when(c > 0)
        def _():
            act(halo(layer, 1, j))

    def halo_waits(layer, j):
        @pl.when(c > 0)
        def _():
            halo(layer, 0, j).wait_recv()

        @pl.when(c < n_cols - 1)
        def _():
            halo(layer, 1, j).wait_recv()

    def frame_copy(h, j):
        return pltpu.make_async_remote_copy(
            src_ref=a2.at[cut(j)],
            dst_ref=x2in.at[h - 1, cut(j)],
            send_sem=z_send.at[h - 1, j],
            recv_sem=z_recv.at[h - 1, j],
            device_id={"tm": k + h},
            device_id_type=MESH,
        )

    def frame_sends(j, act):
        for h in range(1, hops + 1):

            @pl.when(k + h < last)
            def _():
                act(frame_copy(h, j))

    def part_copy(which, j):
        return pltpu.make_async_remote_copy(
            src_ref=(ps if which else qs).at[cut(j)],
            dst_ref=(pr if which else qr).at[cut(j)],
            send_sem=q_send.at[which, j],
            recv_sem=q_recv.at[which, j],
            device_id={"tm": k + 1},
            device_id_type=MESH,
        )

    def out_copy(which, j):
        src = (a1, a2, a3, a4)[which]
        return pltpu.make_async_copy(src.at[cut(j)], outs[which].at[0, cut(j)], o_sem.at[which, j])

    def build(layer, j):
        src, hal, dst = (a1, hal2, s2) if layer else (x, hal1, s1)
        mid = silu(src[cut(j)])
        left = silu(hal[0, cut(j)][:, TILE - 1 :, :])
        right = silu(hal[1, cut(j)][:, :1, :])
        here = pl.ds(j * R + 1, R)
        dst[here, :, 0:C] = jnp.concatenate([left, mid[:, : W - 1]], axis=1).astype(jnp.bfloat16)
        dst[here, :, C : 2 * C] = mid.astype(jnp.bfloat16)
        dst[here, :, 2 * C : 3 * C] = jnp.concatenate([mid[:, 1:], right], axis=1).astype(jnp.bfloat16)

    def conv(layer, j):
        src, s, kern, bias, dst = (a1, s2, k2, b2, a2) if layer else (x, s1, k1, b1, a1)
        acc = src[cut(j)].reshape(M, C).astype(jnp.float32) + bias[...][None, :]
        for dr in range(3):
            acc = acc + mm(s[pl.ds(j * R + dr, R)].reshape(M, 3 * C), kern[dr])
        dst[cut(j)] = acc.astype(jnp.bfloat16).reshape(R, W, C)

    def load(ref):
        return ref.reshape(M, C)

    def act(values):
        return silu(values).astype(jnp.bfloat16)

    def temporal_own(j):
        def arrive(h):
            @pl.when(k >= h)
            def _():
                frame_copy(h, j).wait_recv()

        def each(values, weight):
            out = mm(values[0] if len(values) == 1 else jnp.concatenate(values, axis=0), weight)
            return [out[i * M : (i + 1) * M] for i in range(len(values))]

        x2 = [load(a2[cut(j)])]
        if hops > 0:
            arrive(1)
            x2.append(load(x2in[0, cut(j)]))
        t2 = [act(values) for values in x2]
        u1 = each(t2, u[1])
        part = u1[0]
        if hops > 0:
            part = part + mm(t2[1], u[0])

        @pl.when(k == last - 1)
        def _():
            qs[cut(j)] = part.astype(jnp.bfloat16).reshape(R, W, C)
            part_copy(0, j).start()

        for h in range(2, hops + 1):
            arrive(h)
            x2.append(load(x2in[h - 1, cut(j)]))
            t2.append(act(x2[h]))
        u2 = each(t2[:3], u[2])
        if hops > 1:
            u1 = u1 + each(t2[2:4], u[1])
            u0 = each(t2[2:5], u[0])
        x3 = []
        for i in range(len(u2)):
            total = x2[i].astype(jnp.float32) + tb1[...][None, :] + u2[i]
            if i + 1 < len(u1):
                total = total + u1[i + 1]
            if i + 2 <= hops:
                total = total + u0[i]
            if i > 0:
                total = jnp.where(k >= i, total, 0.0)
            x3.append(total.astype(jnp.bfloat16))
        t3 = [act(values) for values in x3]
        v1 = each(t3[:2], v[1])
        second = v1[0]
        if len(t3) > 1:
            v0 = each(t3[1:], v[0])
            second = second + v0[0]

        @pl.when(k == last - 1)
        def _():
            ps[cut(j)] = second.astype(jnp.bfloat16).reshape(R, W, C)
            part_copy(1, j).start()

        a3[cut(j)] = x3[0].reshape(R, W, C)
        out_copy(2, j).start()
        total = x3[0].astype(jnp.float32) + tb2[...][None, :] + mm(t3[0], v[2])
        if len(t3) > 1:
            total = total + v1[1]
        if len(t3) > 2:
            total = total + v0[1]
        a4[cut(j)] = total.astype(jnp.bfloat16).reshape(R, W, C)
        out_copy(3, j).start()

    def temporal_last(j):
        x2 = load(a2[cut(j)])
        total = x2.astype(jnp.float32) + mm(act(x2), u[2]) + tb1[...][None, :]
        if n > 1:
            part_copy(0, j).wait_recv()
            total = total + load(qr[cut(j)]).astype(jnp.float32)
        x3 = total.astype(jnp.bfloat16)
        a3[cut(j)] = x3.reshape(R, W, C)
        out_copy(2, j).start()
        total = x3.astype(jnp.float32) + mm(act(x3), v[2]) + tb2[...][None, :]
        if n > 1:
            part_copy(1, j).wait_recv()
            total = total + load(pr[cut(j)]).astype(jnp.float32)
        a4[cut(j)] = total.astype(jnp.bfloat16).reshape(R, W, C)
        out_copy(3, j).start()

    def start(copy):
        copy.start()

    @pl.loop(0, chunks)
    def _(j):
        halo_sends(0, j, start)

    def during(j, body):
        @pl.when((j >= 0) & (j < chunks))
        def _():
            body(j)

    def step_build1(j):
        halo_waits(0, j)
        build(0, j)

    def step_conv1(j):
        conv(0, j)
        halo_sends(1, j, start)
        out_copy(0, j).start()

    def step_build2(j):
        halo_waits(1, j)
        build(1, j)

    def step_conv2(j):
        conv(1, j)
        frame_sends(j, start)
        out_copy(1, j).start()

    def step_temporal(j):
        @pl.when(k < last)
        def _():
            temporal_own(j)

        @pl.when(k == last)
        def _():
            temporal_last(j)

    for load_in in loads:
        load_in.wait()
    lag = jnp.where(k == last - 1, EARLY, LAG)

    @pl.loop(0, chunks + 2 + HALO_LAG + LAG)
    def _(t):
        during(t, step_build1)
        during(t - 1, step_conv1)
        during(t - 1 - HALO_LAG, step_build2)
        during(t - 2 - HALO_LAG, step_conv2)
        during(t - 2 - HALO_LAG - lag, step_temporal)

    @pl.loop(0, chunks)
    def _(j):
        for layer in range(2):
            halo_sends(layer, j, lambda copy: copy.wait_send())
        frame_sends(j, lambda copy: copy.wait_send())
        for which in range(4):
            out_copy(which, j).wait()
        if n > 1:

            @pl.when(k == last - 1)
            def _():
                part_copy(0, j).wait_send()
                part_copy(1, j).wait_send()


def rows_per_chunk(rows):
    return max(r for r in range(1, ROWS + 1) if rows % r == 0)


def on_device(n, n_cols, latent, spatial_one, bias_one, spatial_two, bias_two, temporal_one, tbias_one, temporal_two, tbias_two):
    _, rows, W, C = latent.shape
    R = rows_per_chunk(rows)
    chunks = rows // R
    hops = max(0, min(4, n - 2))
    slots = max(1, hops)
    bf = jnp.bfloat16
    block = pltpu.VMEM((rows, W, C), bf)
    dma = pltpu.SemaphoreType.DMA
    anywhere = pl.BlockSpec(memory_space=pl.ANY)
    out = jax.ShapeDtypeStruct(latent.shape, bf)
    args = (
        latent,
        spatial_one.reshape(3, 3 * C, C), bias_one,
        spatial_two.reshape(3, 3 * C, C), bias_two,
        temporal_one, tbias_one, temporal_two, tbias_two,
    )
    results = pl.pallas_call(
        functools.partial(kernel, n, n_cols, R, hops),
        out_shape=(out,) * 4,
        in_specs=[anywhere] * 9,
        out_specs=(anywhere,) * 4,
        scratch_shapes=[
            *(pltpu.VMEM(arg.shape, arg.dtype) for arg in args),
            pltpu.VMEM((2, rows, TILE, C), bf),
            pltpu.VMEM((2, rows, TILE, C), bf),
            pltpu.VMEM((rows + 2, W, 3 * C), bf),
            pltpu.VMEM((rows + 2, W, 3 * C), bf),
            pltpu.VMEM((slots, rows, W, C), bf),
            block, block, block, block,
            block, block, block, block,
            dma((2, 2, chunks)), dma((2, 2, chunks)),
            dma((slots, chunks)), dma((slots, chunks)),
            dma((2, chunks)), dma((2, chunks)),
            dma((9,)), dma((4, chunks)),
        ],
        compiler_params=pltpu.CompilerParams(
            collective_id=0, has_side_effects=True, vmem_limit_bytes=VMEM_BYTES
        ),
    )(*args)
    return pl.pallas_call(
        write_out,
        out_shape=(out,) * 4,
        in_specs=[anywhere] * 4,
        out_specs=(anywhere,) * 4,
        scratch_shapes=[
            *(pltpu.VMEM(latent.shape, bf) for _ in range(4)),
            dma((4, PIECES)), dma((4, PIECES)),
        ],
        compiler_params=pltpu.CompilerParams(vmem_limit_bytes=VMEM_BYTES),
    )(*results)


def write_out(*refs):
    given, outs, held, i_sem, o_sem = refs[:4], refs[4:8], refs[8:12], refs[12], refs[13]
    rows = given[0].shape[1]
    ins, back = [], []
    for p in range(PIECES):
        part = pl.ds(rows * p // PIECES, rows * (p + 1) // PIECES - rows * p // PIECES)
        for i in range(4):
            ins.append(pltpu.make_async_copy(given[i].at[:, part], held[i].at[:, part], i_sem.at[i, p]))
            back.append(pltpu.make_async_copy(held[i].at[:, part], outs[i].at[:, part], o_sem.at[i, p]))
    for copy in ins:
        copy.start()
    for copy, after in zip(ins, back):
        copy.wait()
        after.start()
    for copy in back:
        copy.wait()


def solution(mesh):
    spec = P(("groups", "tm"), None, "cols", None)
    return jax.shard_map(
        functools.partial(on_device, mesh.shape["tm"], mesh.shape["cols"]),
        mesh=mesh,
        in_specs=(spec, P(), P(), P(), P(), P(), P(), P(), P()),
        out_specs=(spec,) * 4,
        check_vma=False,
    )
```
